256 devices in a mesh: dom: 64 (over z, y, core), hid: 4 (over x).
Axes of the slice: x: 4, y: 4, z: 8, core: 2. Of those that a mesh axis runs over, the one named last changes fastest.
Arguments:
- node_features: bfloat16 [262144, 512], P('dom', 'hid'), may hold values from -6 to 6
- weight: bfloat16 [512, 512], P(None, 'hid'), may hold values from -0.25 to 0.25
- adjacency_tiles: bfloat16 [11264, 128, 128], P('dom'), may hold values from -0.25 to 0.25
- tile_rows: int32 [64, 176], P('dom'), may hold values from 0 to 31, as said below
- tile_cols: int32 [64, 176], P('dom'), may hold values from 0 to 95, as said below
- tile_count: int32 [64], P('dom'), may hold values from 33 to 176
- send_blocks: int32 [64, 64], P('dom'), may hold values from 0 to 31
- activation_bits: int32 [262144, 32], P('dom', 'hid'), may hold values from 0 to 65535, as said below
- out_cotangent: bfloat16 [262144, 512], P('dom', 'hid'), may hold values from -6 to 6
Outputs:
- out_act: bfloat16 [262144, 512], P('dom', 'hid')
- input_grad: bfloat16 [262144, 512], P('dom', 'hid')
- weight_grad: float32 [512, 512], P(None, 'hid')
The draws below stay inside these ranges and needn't reach their ends.
Inputs may be any that keep to these rules, and one draw needn't show every extreme that they name: `tile_rows`: the first 32 tiles of every partition have row block i and source i, for i below 32. `tile_cols`: no tile of partition p names 32 + p. `activation_bits`: every word holds 16 independent bits.
All inputs are finite; a program needn't handle non-finite values.
Results may differ from the reference program's by a relative error of at most 0.005.
Values may be sent and summed in bfloat16 or wider, within the bound.
No kernel may reach another device: no remote copies, remote signals or barrier semaphores. Data moves between devices by JAX's collectives and lax.ppermute only.
A program may use at most 128 MiB of HBM per device.

```python
import jax
import jax.numpy as jnp
from jax import lax

D = 512
BLOCK = 128
RB = 32
T_MAX = 176
PARTITIONS = 64
NODES = 262144
TILE_ALL = 11264
WORDS = 32


def draw_tile_rows(key, part):
    key = jax.random.fold_in(key, 1)
    diagonal = jnp.broadcast_to(jnp.arange(RB, dtype=jnp.int32)[None, :], (PARTITIONS, RB))
    extra = jax.random.randint(key, (PARTITIONS, T_MAX - RB), 0, RB, dtype=jnp.int32)
    return jnp.concatenate([diagonal, extra], 1)


def draw_tile_cols(key, part):
    key = jax.random.fold_in(key, 2)
    key_kind, key_local, key_offset = jax.random.split(key, 3)
    kinds = jax.random.randint(key_kind, (PARTITIONS, T_MAX - RB), 0, 4, dtype=jnp.int32)
    local_cols = jax.random.randint(key_local, (PARTITIONS, T_MAX - RB), 0, RB, dtype=jnp.int32)
    offsets = jax.random.randint(key_offset, (PARTITIONS, T_MAX - RB), 1, PARTITIONS, dtype=jnp.int32)
    peer_ids = (jnp.arange(PARTITIONS, dtype=jnp.int32)[:, None] + offsets) % PARTITIONS
    extra = jnp.where(kinds < 3, RB + peer_ids, local_cols)
    extra = extra.at[0, 0].set(RB + PARTITIONS - 1)
    diagonal = jnp.broadcast_to(jnp.arange(RB, dtype=jnp.int32)[None, :], (PARTITIONS, RB))
    return jnp.concatenate([diagonal, extra], 1).astype(jnp.int32)


def draw_tile_count(key, part):
    key = jax.random.fold_in(key, 3)
    key_level, key_busy = jax.random.split(key, 2)
    levels = jax.random.randint(key_level, (PARTITIONS,), 0, 9, dtype=jnp.int32)
    counts = RB + 1 + levels * levels * (T_MAX - RB - 1) // 64
    busiest = jax.random.randint(key_busy, (), 0, PARTITIONS, dtype=jnp.int32)
    counts = counts.at[busiest].set(T_MAX)
    counts = counts.at[(busiest + 1) % PARTITIONS].set(RB + 1)
    return counts.astype(jnp.int32)


def draw_send_blocks(key, part):
    key = jax.random.fold_in(key, 4)
    chosen = jax.random.randint(key, (PARTITIONS, PARTITIONS), 0, RB, dtype=jnp.int32)
    chosen = chosen.at[0, 1].set(RB - 1)
    chosen = chosen.at[1, 0].set(0)
    return chosen


def draw_activation_bits(key, part):
    key = jax.random.fold_in(key, 5)
    words = jax.random.randint(key, (NODES, WORDS), 0, 65536, dtype=jnp.int32)
    words = words.at[0, 0].set(jnp.int32(65535))
    words = words.at[1, 0].set(jnp.int32(0))
    return words


def block_levels(rng, shape, cuts, least, largest):
    factor_of, own = 1.0, jax.random.fold_in(rng, 6)
    for dim, parts in cuts:
        heights = jnp.exp(jax.random.uniform(jax.random.fold_in(own, dim), (parts,), jnp.float32, least / len(cuts), largest / len(cuts)))
        factor_of = factor_of * jnp.repeat(heights, shape[dim] // parts).reshape([-1 if axis == dim else 1 for axis in range(len(shape))])
    return factor_of


def normal_values(own_key, shape, scale, limit, pieces=(), kind=jnp.bfloat16):
    gain = block_levels(own_key, shape, pieces, -0.22, 0.18) if pieces else 1.0
    drawn = jax.random.normal(own_key, shape, jnp.float32) * scale * gain
    return jnp.minimum(jnp.maximum(drawn, -limit), limit).astype(kind)


def setup_inputs(seed: int = 0) -> dict:
    arg_keys = jax.random.split(jax.random.key(seed), 10)
    node_features = normal_values(arg_keys[0], (NODES, D), 1.0, 6.0, ((0, 64), (1, 4)))
    weight = normal_values(arg_keys[1], (D, D), D ** -0.5, 0.25, ((1, 4),))
    adjacency_tiles = normal_values(arg_keys[2], (TILE_ALL, BLOCK, BLOCK), (4 * BLOCK) ** -0.5, 0.25, ((0, 64),))
    tile_rows = draw_tile_rows(jax.random.fold_in(arg_keys[9], 71), 0)
    tile_cols = draw_tile_cols(jax.random.fold_in(arg_keys[9], 71), 0)
    tile_count = draw_tile_count(jax.random.fold_in(arg_keys[9], 71), 0)
    send_blocks = draw_send_blocks(jax.random.fold_in(arg_keys[9], 71), 0)
    activation_bits = draw_activation_bits(jax.random.fold_in(arg_keys[9], 71), 0)
    out_cotangent = normal_values(arg_keys[8], (NODES, D), 1.0, 6.0, ((0, 64), (1, 4)))
    return dict(node_features=node_features, weight=weight, adjacency_tiles=adjacency_tiles, tile_rows=tile_rows, tile_cols=tile_cols, tile_count=tile_count, send_blocks=send_blocks, activation_bits=activation_bits, out_cotangent=out_cotangent)


def unpack_bits(packed):
    shifts = jnp.arange(16, dtype=jnp.int32)
    bit_flags = jnp.right_shift(packed[:, :, None], shifts) & 1
    return bit_flags.reshape(packed.shape[0], packed.shape[1] * 16) > 0


def reference(node_features, weight, adjacency_tiles, tile_rows, tile_cols, tile_count, send_blocks, activation_bits, out_cotangent):
    hidden = jnp.dot(node_features, weight, preferred_element_type=jnp.float32).astype(jnp.bfloat16)
    hidden_blocks = hidden.reshape(PARTITIONS, RB, BLOCK, D)
    tile_data = adjacency_tiles.reshape(PARTITIONS, T_MAX, BLOCK, BLOCK)
    in_list = (jnp.arange(T_MAX, dtype=jnp.int32)[None, :] < tile_count[:, None]).astype(jnp.float32)
    peers = jnp.arange(PARTITIONS, dtype=jnp.int32)

    def forward_one(partition):
        own_blocks = hidden_blocks[partition]
        incoming = hidden_blocks[peers, send_blocks[:, partition]]
        sources = jnp.concatenate([own_blocks, incoming], 0)
        picked = sources[tile_cols[partition]]
        products = jnp.einsum('tij,tjk->tik', tile_data[partition].astype(jnp.float32), picked.astype(jnp.float32))
        products = products * in_list[partition][:, None, None]
        return jax.ops.segment_sum(products, tile_rows[partition], num_segments=RB)

    aggregated = lax.map(forward_one, peers).reshape(NODES, D)
    active = unpack_bits(activation_bits)
    out_act = jnp.where(active, aggregated, jnp.float32(0.0)).astype(jnp.bfloat16)
    d_aggregated = jnp.where(active, out_cotangent, jnp.zeros_like(out_cotangent))
    d_blocks = d_aggregated.reshape(PARTITIONS, RB, BLOCK, D)

    def backward_one(accumulated, partition):
        picked = d_blocks[partition][tile_rows[partition]]
        products = jnp.einsum('tji,tjk->tik', tile_data[partition].astype(jnp.float32), picked.astype(jnp.float32))
        products = products * in_list[partition][:, None, None]
        slot_sums = jax.ops.segment_sum(products, tile_cols[partition], num_segments=RB + PARTITIONS)
        accumulated = accumulated.at[partition].add(slot_sums[:RB])
        accumulated = accumulated.at[peers, send_blocks[:, partition]].add(slot_sums[RB:])
        return accumulated, None

    start_sums = jnp.zeros((PARTITIONS, RB, BLOCK, D), jnp.float32)
    d_sums, unused_out = lax.scan(backward_one, start_sums, peers)
    d_hidden = d_sums.reshape(NODES, D).astype(jnp.bfloat16)
    weight_grad = jnp.dot(node_features.T, d_hidden, preferred_element_type=jnp.float32)
    input_grad = jnp.dot(d_hidden, weight.T, preferred_element_type=jnp.float32).astype(jnp.bfloat16)
    return out_act, input_grad, weight_grad
```

```python
import functools

import jax
import jax.numpy as jnp
from jax import lax
from jax.experimental import pallas as pl
from jax.experimental.pallas import tpu as pltpu
from jax.sharding import PartitionSpec as P

B = 128
RB = 32
HID = 4
CHUNK = RB // HID
F32 = jnp.float32
BF16 = jnp.bfloat16
LIMIT = 60 * 1024 * 1024

VMEM = pl.BlockSpec(memory_space=pltpu.VMEM)
SMEM = pl.BlockSpec(memory_space=pltpu.SMEM)
ANY = pl.BlockSpec(memory_space=pl.ANY)
HBM = pl.BlockSpec(memory_space=pltpu.HBM)


def params():
    return pltpu.CompilerParams(vmem_limit_bytes=LIMIT)


def cost(flops, nbytes):
    return pl.CostEstimate(flops=flops, bytes_accessed=nbytes, transcendentals=0)


def dot(a, b, dims=((1,), (0,))):
    return lax.dot_general(a, b, (dims, ((), ())), preferred_element_type=F32)


def rel(me, shift):
    return lax.rem(me + shift + HID, HID)


def bit_mask(words):
    halves = jnp.concatenate([words & 255, words >> 8], 0).astype(F32).astype(BF16)
    row = lax.broadcasted_iota(jnp.int32, (16, B), 0)
    unit = lax.broadcasted_iota(jnp.int32, (16, B), 1)
    byte_row = (unit // 16) + 8 * ((unit % 16) // 8)
    scale = lax.div(jnp.ones((16, B), F32), (1 << (unit % 8)).astype(F32))
    spread = jnp.where(row == byte_row, scale, 0.0).astype(BF16)
    shifted = dot(halves, spread, ((0,), (0,)))
    return (shifted.astype(jnp.int32) & 1) == 1


STEP = 256
TILES = 176
PIECES = 4
PIECE = TILES // PIECES
INNER = PIECE // 4


def tile_copies(tiles_hbm, tiles, sems):
    return [
        pltpu.make_async_copy(
            tiles_hbm.at[pl.ds(k * PIECE, PIECE)], tiles.at[pl.ds(k * PIECE, PIECE)], sems.at[k]
        )
        for k in range(PIECES)
    ]


def tiles_bwd_kernel(count_ref, rows_ref, cols_ref, bits_hbm, cot_hbm, tiles_hbm, own_hbm,
                     slot_hbm, tiles, bits, cot, d_t, acc, slots, sems, out_sems):
    count = count_ref[0]
    bits_in = pltpu.make_async_copy(bits_hbm, bits, sems.at[PIECES])
    cot_in = pltpu.make_async_copy(cot_hbm, cot, sems.at[PIECES + 1])
    bits_in.start()
    cot_in.start()
    copies = tile_copies(tiles_hbm, tiles, sems)
    for c in copies:
        c.start()
    acc[...] = jnp.zeros_like(acc)
    bits_in.wait()
    cot_in.wait()

    def mask(i, carry):
        at = pl.multiple_of(i * STEP, STEP)
        active = bit_mask(bits[:, pl.ds(at, STEP)])
        v = jnp.where(active, cot[pl.ds(at, STEP), :].astype(F32), 0.0)
        for j in range(STEP // B):
            d_t[i * (STEP // B) + j] = v[j * B : (j + 1) * B].T.astype(BF16)
        return carry

    lax.fori_loop(0, 4096 // STEP, mask, 0)
    for k in range(PIECES):
        copies[k].wait()

        def body(i, carry, k=k):
            for j in range(INNER):
                t = k * PIECE + i * INNER + j
                s = jnp.where(t < count, cols_ref[0, t], RB + 64)
                acc[s] += dot(d_t[rows_ref[0, t]], tiles[t])
            return carry

        lax.fori_loop(0, 4, body, 0)
    outs = []
    for k in range(4):
        at = pl.ds(k * 16, 16)
        slots[at] = acc[RB + k * 16 : RB + (k + 1) * 16].astype(BF16)
        outs.append(pltpu.make_async_copy(slots.at[at], slot_hbm.at[at], out_sems.at[k]))
        outs[-1].start()
    outs.append(pltpu.make_async_copy(acc.at[pl.ds(0, RB)], own_hbm, out_sems.at[4]))
    outs[-1].start()
    for c in outs:
        c.wait()


def tiles_bwd_call(count, rows, cols, bits_t, cot, tiles):
    return pl.pallas_call(
        tiles_bwd_kernel,
        out_shape=[
            jax.ShapeDtypeStruct((RB, B, B), F32),
            jax.ShapeDtypeStruct((64, B, B), BF16),
        ],
        in_specs=[SMEM] * 3 + [ANY] * 3,
        out_specs=[HBM] * 2,
        scratch_shapes=[
            pltpu.VMEM((TILES, B, B), BF16),
            pltpu.VMEM((8, 4096), jnp.int32),
            pltpu.VMEM((4096, B), BF16),
            pltpu.VMEM((RB, B, B), BF16),
            pltpu.VMEM((RB + 65, B, B), F32),
            pltpu.VMEM((64, B, B), BF16),
            pltpu.SemaphoreType.DMA((PIECES + 2,)),
            pltpu.SemaphoreType.DMA((5,)),
        ],
        compiler_params=params(),
        cost_estimate=cost(2 * TILES * B * B * B, 30 << 20),
        name="tiles_bwd",
    )(count, rows, cols, bits_t, cot, tiles)


def tiles_fwd_kernel(count_ref, rows_ref, cols_ref, bits_ref, own_hbm, recv_hbm, tiles_hbm,
                     after, out_ref, tiles, src, acc, sems):
    count = count_ref[0]
    own = pltpu.make_async_copy(own_hbm, src.at[pl.ds(0, RB)], sems.at[PIECES])
    got = pltpu.make_async_copy(recv_hbm, src.at[pl.ds(RB, 64)], sems.at[PIECES + 1])
    own.start()
    got.start()
    copies = tile_copies(tiles_hbm, tiles, sems)
    for c in copies:
        c.start()
    acc[...] = jnp.zeros_like(acc)
    own.wait()
    got.wait()
    for k in range(PIECES):
        copies[k].wait()

        def body(i, carry, k=k):
            for j in range(INNER):
                t = k * PIECE + i * INNER + j
                r = jnp.where(t < count, rows_ref[0, t], RB)
                acc[r] += dot(tiles[t], src[cols_ref[0, t]])
            return carry

        lax.fori_loop(0, 4, body, 0)

    def mask(i, carry):
        at = pl.multiple_of(i * STEP, STEP)
        active = bit_mask(bits_ref[:, pl.ds(at, STEP)])
        for j in range(STEP // B):
            b = i * (STEP // B) + j
            out_ref[b] = jnp.where(active[j * B : (j + 1) * B], acc[b], 0.0).astype(BF16)
        return carry

    lax.fori_loop(0, 4096 // STEP, mask, 0)


def tiles_fwd_call(count, rows, cols, bits_t, own, recv, tiles, after):
    return pl.pallas_call(
        tiles_fwd_kernel,
        out_shape=jax.ShapeDtypeStruct((RB, B, B), BF16),
        in_specs=[SMEM] * 3 + [VMEM] + [ANY] * 4,
        out_specs=VMEM,
        scratch_shapes=[
            pltpu.VMEM((TILES, B, B), BF16),
            pltpu.VMEM((RB + 64, B, B), BF16),
            pltpu.VMEM((RB + 1, B, B), F32),
            pltpu.SemaphoreType.DMA((PIECES + 2,)),
        ],
        compiler_params=params(),
        cost_estimate=cost(2 * TILES * B * B * B, 30 << 20),
        name="tiles_fwd",
    )(count, rows, cols, bits_t, own, recv, tiles, after)


def hidden_kernel(me_ref, send_ref, x0, x1, x2a, x2b, x3, w_ref, w1, w2, w3, hid_hbm, out_hbm, hid, sems):
    me = me_ref[0]
    rhs = jnp.concatenate(
        [w_ref[pl.ds(pl.multiple_of(rel(me, -s) * B, B), B), :] for s in range(HID)], 0
    )
    for n in range(4096 // STEP):
        half, at = (x2a, n * STEP) if n < 2048 // STEP else (x2b, n * STEP - 2048)
        here = slice(n * STEP, (n + 1) * STEP)
        lhs = jnp.concatenate([x0[here, :], x1[here, :], half[at : at + STEP, :], x3[here, :]], 1)
        r = dot(lhs, rhs).astype(BF16)
        for j in range(STEP // B):
            hid[n * (STEP // B) + j] = r[j * B : (j + 1) * B]
    copies = [
        pltpu.make_async_copy(hid.at[send_ref[0, q]], out_hbm.at[q], sems.at[q]) for q in range(64)
    ]
    copies.append(pltpu.make_async_copy(hid, hid_hbm, sems.at[64]))
    for c in copies:
        c.start()
    for c in copies:
        c.wait()


def hidden_call(me, send, xs, w, ws):
    return pl.pallas_call(
        hidden_kernel,
        out_shape=[
            jax.ShapeDtypeStruct((RB, B, B), BF16),
            jax.ShapeDtypeStruct((64, B, B), BF16),
        ],
        in_specs=[SMEM] * 2 + [VMEM] * 6 + [ANY] * 3,
        out_specs=[HBM] * 2,
        scratch_shapes=[pltpu.VMEM((RB, B, B), BF16), pltpu.SemaphoreType.DMA((65,))],
        compiler_params=params(),
        cost_estimate=cost(2 * 4096 * 512 * 128, 10 << 20),
        name="hidden",
    )(me, send, *xs, w, *ws[1:])


def sum_kernel(me_ref, send_ref, own_hbm, got_hbm, x0, x1, x2a, x2b, x3, after, terms_hbm, d_hbm,
               acc, got, xv, flat, dv, terms, sems, out_sems):
    me, y = me_ref[0], me_ref[1]
    ins = [
        pltpu.make_async_copy(own_hbm, acc, sems.at[0]),
        pltpu.make_async_copy(got_hbm, got, sems.at[1]),
        pltpu.make_async_copy(x0, xv.at[0], sems.at[2]),
        pltpu.make_async_copy(x1, xv.at[1], sems.at[3]),
        pltpu.make_async_copy(x2a, xv.at[2, pl.ds(0, 2048)], sems.at[4]),
        pltpu.make_async_copy(x2b, xv.at[2, pl.ds(2048, 2048)], sems.at[5]),
        pltpu.make_async_copy(x3, xv.at[3], sems.at[6]),
    ]
    for i in ins:
        i.start()
    ins[0].wait()
    ins[1].wait()

    def body(i, carry):
        for j in range(8):
            q = i * 8 + j
            acc[send_ref[0, q]] += got[q].astype(F32)
        return carry

    lax.fori_loop(0, 8, body, 0)
    outs = []

    def flip(i, carry):
        for j in range(4):
            dv[i * 4 + j] = acc[i * 4 + j].T.astype(BF16)
        return carry

    for k in range(4):
        at = pl.ds(k * CHUNK, CHUNK)
        lax.fori_loop(2 * k, 2 * k + 2, flip, 0)
        outs.append(pltpu.make_async_copy(dv.at[at], d_hbm.at[at], out_sems.at[k]))
        outs[-1].start()
    for b in range(RB):
        flat[:, b * B : (b + 1) * B] = acc[b].astype(BF16)
    for i in ins[2:]:
        i.wait()
    for s in range(HID):
        r = dot(flat[...], xv[s]).T
        terms[pl.ds(pl.multiple_of(rel(me, -s) * B, B), B), :] = r
    for k in range(4):
        at = pl.multiple_of(lax.rem(y + k, 4) * B, B)
        outs.append(
            pltpu.make_async_copy(
                terms.at[pl.ds(at, B)], terms_hbm.at[pl.ds(k * B, B)], out_sems.at[4 + k]
            )
        )
        outs[-1].start()
    for o in outs:
        o.wait()


def sum_call(me, send, own, got, xs, after):
    return pl.pallas_call(
        sum_kernel,
        out_shape=[jax.ShapeDtypeStruct((512, B), F32)]
        + [jax.ShapeDtypeStruct((RB, B, B), BF16)],
        in_specs=[SMEM] * 2 + [ANY] * 8,
        out_specs=[HBM] * 2,
        scratch_shapes=[
            pltpu.VMEM((RB, B, B), F32),
            pltpu.VMEM((64, B, B), BF16),
            pltpu.VMEM((HID, 4096, B), BF16),
            pltpu.VMEM((B, 4096), BF16),
            pltpu.VMEM((RB, B, B), BF16),
            pltpu.VMEM((512, B), F32),
            pltpu.SemaphoreType.DMA((7,)),
            pltpu.SemaphoreType.DMA((8,)),
        ],
        compiler_params=params(),
        cost_estimate=cost(2 * 4096 * 512 * 128, 12 << 20),
        name="sum_returned",
    )(me, send, own, got, *xs, after)


def add_kernel(a, b, c, d, out):
    out[...] = ((a[...] + b[...]) + (c[...] + d[...])).astype(BF16)


def add_call(parts):
    return pl.pallas_call(
        add_kernel,
        out_shape=jax.ShapeDtypeStruct((B, B), BF16),
        in_specs=[VMEM] * 4,
        out_specs=VMEM,
        compiler_params=params(),
        cost_estimate=cost(4 * B * B, 1 << 18),
        name="add_y",
    )(*parts)


def add_z_kernel(me_ref, *refs):
    parts, out, by_z = refs[:8], refs[8], refs[9]
    z = me_ref[2]
    for k in range(8):
        by_z[lax.rem(z + 8 - k, 8)] = parts[k][...].astype(F32)
    total = by_z[0]
    for k in range(1, 8):
        total = total + by_z[k]
    out[...] = total


def add_z_call(me, parts):
    return pl.pallas_call(
        add_z_kernel,
        out_shape=jax.ShapeDtypeStruct((B, B), F32),
        in_specs=[SMEM] + [VMEM] * 8,
        out_specs=VMEM,
        scratch_shapes=[pltpu.VMEM((8, B, B), F32)],
        compiler_params=params(),
        cost_estimate=cost(8 * B * B, 1 << 19),
        name="add_z",
    )(me, *parts)


def round_y_kernel(me_ref, t0, t1, t2, t3, after, out):
    for k, t in enumerate((t0, t1, t2, t3)):
        out[pl.ds(pl.multiple_of(rel(me_ref[1], -k) * B, B), B), :] = t[...]


def round_y_call(me, parts, after):
    return pl.pallas_call(
        round_y_kernel,
        out_shape=jax.ShapeDtypeStruct((512, B), F32),
        in_specs=[SMEM] + [VMEM] * 4 + [ANY],
        out_specs=VMEM,
        compiler_params=params(),
        cost_estimate=cost(512 * B, 1 << 19),
        name="round_y",
    )(me, *parts, after)


def back_kernel(d0, d1, d2a, d2b, d3, w0, w1, w2, w3, after, out_hbm, d, out, sems, out_sems):
    parts = [pl.ds(k * 1024, 1024) for k in range(4)]
    ins = []
    for k, p in enumerate(parts):
        half = pl.ds((k % 2) * 1024, 1024)
        for s, v in enumerate((d0.at[p], d1.at[p], (d2a, d2b)[k // 2].at[half], d3.at[p])):
            ins.append(pltpu.make_async_copy(v, d.at[s, p], sems.at[len(ins)]))
    outs = [
        pltpu.make_async_copy(out.at[p], out_hbm.at[p], out_sems.at[k])
        for k, p in enumerate(parts)
    ]
    for c in ins:
        c.start()
    rhs = jnp.concatenate([w0[...], w1[...], w2[...], w3[...]], 1)
    for k in range(4):
        for c in ins[4 * k : 4 * k + 4]:
            c.wait()
        for n in range(1024 // STEP):
            at = slice(k * 1024 + n * STEP, k * 1024 + (n + 1) * STEP)
            lhs = jnp.concatenate([d[s, at, :] for s in range(HID)], 1)
            out[at, :] = dot(lhs, rhs, ((1,), (1,))).astype(BF16)
        outs[k].start()
    for c in outs:
        c.wait()


def back_call(ds, ws, after):
    return pl.pallas_call(
        back_kernel,
        out_shape=jax.ShapeDtypeStruct((4096, B), BF16),
        in_specs=[ANY] * 5 + [VMEM] * HID + [ANY],
        out_specs=HBM,
        scratch_shapes=[
            pltpu.VMEM((HID, 4096, B), BF16),
            pltpu.VMEM((4096, B), BF16),
            pltpu.SemaphoreType.DMA((16,)),
            pltpu.SemaphoreType.DMA((4,)),
        ],
        compiler_params=params(),
        cost_estimate=cost(2 * 4096 * 512 * 128, 5 << 20),
        name="d_times_wt",
    )(*ds, *ws, after)


def shift_hid(v, s):
    return lax.ppermute(v, "hid", [(i, (i + s) % HID) for i in range(HID)])


def split_kernel(v1, v3, after, low, high):
    low[...] = v1[...]
    high[...] = v3[...]


def split_call(v1, v3, after):
    half = jax.ShapeDtypeStruct((2048, B), BF16)
    return pl.pallas_call(
        split_kernel,
        out_shape=[half] * 2,
        grid=(1,),
        in_specs=[
            pl.BlockSpec((2048, B), lambda i: (0, 0)),
            pl.BlockSpec((2048, B), lambda i: (1, 0)),
            ANY,
        ],
        out_specs=[pl.BlockSpec((2048, B), lambda i: (0, 0))] * 2,
        compiler_params=params(),
        cost_estimate=cost(1000, 2 << 20),
        name="halves",
    )(v1, v3, after)


def gather_hid(v, after):
    v1, v3 = shift_hid(v, 1), shift_hid(v, 3)
    low, high = split_call(v1, v3, after)
    return v, v1, shift_hid(low, 1), shift_hid(high, 3), v3


def shift_dom(v, dz, dy, dc):
    pairs = [
        ((z * 4 + y) * 2 + c, (((z + dz) % 8) * 4 + (y + dy) % 4) * 2 + (c ^ dc))
        for z in range(8)
        for y in range(4)
        for c in range(2)
    ]
    return lax.ppermute(v, "dom", pairs)


def all_to_all(v):
    return lax.all_to_all(v, "dom", split_axis=0, concat_axis=0, tiled=True)


def per_device(x, w, tiles, rows, cols, count, send, bits, cot):
    hid = lax.axis_index("hid").astype(jnp.int32)
    dom = lax.axis_index("dom").astype(jnp.int32)
    z, y = dom // 8, (dom // 2) % 4
    me = jnp.stack([hid, y, z])
    bits_t = bits.T

    own, slots = tiles_bwd_call(count, rows, cols, bits_t, cot, tiles)
    returned = all_to_all(slots)

    xs = gather_hid(x, slots)
    ws = [lax.dynamic_slice_in_dim(w, ((hid + s) % HID) * B, B) for s in range(HID)]
    ws = [ws[0]] + [shift_hid(ws[s], s) for s in range(1, HID)]
    hidden, outgoing = hidden_call(me, send, xs, w, ws)
    incoming = all_to_all(outgoing)

    terms, d = sum_call(me, send, own, returned, xs, outgoing)
    terms = (terms + shift_dom(terms, 0, 0, 1)).reshape(4, B, B)
    terms = [terms[0]] + [shift_dom(terms[k], 0, k, 0) for k in (1, 3, 2)]
    part = add_call(terms)
    ds = gather_hid(d.reshape(4096, B), part)
    total = add_z_call(me, [part] + [shift_dom(part, k, 0, 0) for k in range(1, 8)])
    out_act = tiles_fwd_call(count, rows, cols, bits_t, hidden, incoming, tiles, total)
    input_grad = back_call(ds, ws, out_act)
    total = [total] + [shift_dom(total, 0, k, 0) for k in range(1, 4)]
    weight_grad = round_y_call(me, total, out_act)
    return out_act.reshape(4096, B), input_grad, weight_grad


def solution(mesh):
    placed = (
        P("dom", "hid"),
        P(None, "hid"),
        P("dom", None, None),
        P("dom", None),
        P("dom", None),
        P("dom"),
        P("dom", None),
        P("dom", "hid"),
        P("dom", "hid"),
    )
    return jax.shard_map(
        per_device,
        mesh=mesh,
        in_specs=placed,
        out_specs=(P("dom", "hid"), P("dom", "hid"), P(None, "hid")),
        check_vma=False,
    )
```

```python
import functools

import jax
import jax.numpy as jnp
from jax import lax
from jax.experimental import pallas as pl
from jax.experimental.pallas import tpu as pltpu
from jax.sharding import PartitionSpec as P

B = 128
RB = 32
HID = 4
CHUNK = RB // HID
F32 = jnp.float32
BF16 = jnp.bfloat16
MIB = 1024 * 1024

VMEM = pl.BlockSpec(memory_space=pltpu.VMEM)
SMEM = pl.BlockSpec(memory_space=pltpu.SMEM)
ANY = pl.BlockSpec(memory_space=pl.ANY)
HBM = pl.BlockSpec(memory_space=pltpu.HBM)


def params(mib=60):
    return pltpu.CompilerParams(vmem_limit_bytes=mib * MIB)


def cost(flops, nbytes):
    return pl.CostEstimate(flops=flops, bytes_accessed=nbytes, transcendentals=0)


def dot(a, b, dims=((1,), (0,))):
    return lax.dot_general(a, b, (dims, ((), ())), preferred_element_type=F32)


def rel(me, shift):
    return lax.rem(me + shift + HID, HID)


def bit_mask(words):
    halves = jnp.concatenate([words & 255, words >> 8], 0).astype(F32).astype(BF16)
    row = lax.broadcasted_iota(jnp.int32, (16, B), 0)
    unit = lax.broadcasted_iota(jnp.int32, (16, B), 1)
    byte_row = (unit // 16) + 8 * ((unit % 16) // 8)
    scale = lax.div(jnp.ones((16, B), F32), (1 << (unit % 8)).astype(F32))
    spread = jnp.where(row == byte_row, scale, 0.0).astype(BF16)
    shifted = dot(halves, spread, ((0,), (0,)))
    return (shifted.astype(jnp.int32) & 1) == 1


STEP = 256
MASK_STEP = 1024
TILES = 176
PIECES = 4
PIECE = TILES // PIECES


def tile_copies(tiles_hbm, tiles, sems):
    return [
        pltpu.make_async_copy(
            tiles_hbm.at[pl.ds(k * PIECE, PIECE)], tiles.at[pl.ds(k * PIECE, PIECE)], sems.at[k]
        )
        for k in range(PIECES)
    ]


def tiles_bwd_kernel(count_ref, rows_ref, cols_ref, bits_hbm, cot_hbm, tiles_hbm, own_hbm,
                     slot_hbm, tiles, bits, cot, d_t, acc, slots, sems, out_sems):
    count = count_ref[0]
    bits_in = pltpu.make_async_copy(bits_hbm, bits, sems.at[PIECES])
    cot_in = pltpu.make_async_copy(cot_hbm, cot, sems.at[PIECES + 1])
    bits_in.start()
    cot_in.start()
    copies = tile_copies(tiles_hbm, tiles, sems)
    for c in copies:
        c.start()
    acc[...] = jnp.zeros_like(acc)
    bits_in.wait()
    cot_in.wait()

    def mask(i, carry):
        at = pl.multiple_of(i * MASK_STEP, MASK_STEP)
        active = bit_mask(bits[:, pl.ds(at, MASK_STEP)])
        v = jnp.where(active, cot[pl.ds(at, MASK_STEP), :].astype(F32), 0.0)
        for j in range(MASK_STEP // B):
            d_t[i * (MASK_STEP // B) + j] = v[j * B : (j + 1) * B].T.astype(BF16)
        return carry

    lax.fori_loop(0, 4096 // MASK_STEP, mask, 0)
    for k in range(PIECES):
        copies[k].wait()

        for t in range(k * PIECE, (k + 1) * PIECE):
            s = jnp.where(t < count, cols_ref[0, t], RB + 64)
            acc[s] += dot(d_t[rows_ref[0, t]], tiles[t])
    outs = []
    for k in range(4):
        at = pl.ds(k * 16, 16)
        slots[at] = acc[RB + k * 16 : RB + (k + 1) * 16].astype(BF16)
        outs.append(pltpu.make_async_copy(slots.at[at], slot_hbm.at[at], out_sems.at[k]))
        outs[-1].start()
    outs.append(pltpu.make_async_copy(acc.at[pl.ds(0, RB)], own_hbm, out_sems.at[4]))
    outs[-1].start()
    for c in outs:
        c.wait()


def tiles_bwd_call(count, rows, cols, bits_t, cot, tiles):
    return pl.pallas_call(
        tiles_bwd_kernel,
        out_shape=[
            jax.ShapeDtypeStruct((RB, B, B), F32),
            jax.ShapeDtypeStruct((64, B, B), BF16),
        ],
        in_specs=[SMEM] * 3 + [ANY] * 3,
        out_specs=[HBM] * 2,
        scratch_shapes=[
            pltpu.VMEM((TILES, B, B), BF16),
            pltpu.VMEM((8, 4096), jnp.int32),
            pltpu.VMEM((4096, B), BF16),
            pltpu.VMEM((RB, B, B), BF16),
            pltpu.VMEM((RB + 65, B, B), F32),
            pltpu.VMEM((64, B, B), BF16),
            pltpu.SemaphoreType.DMA((PIECES + 2,)),
            pltpu.SemaphoreType.DMA((5,)),
        ],
        compiler_params=params(),
        cost_estimate=cost(2 * TILES * B * B * B, 30 << 20),
        name="tiles_bwd",
    )(count, rows, cols, bits_t, cot, tiles)


def tiles_fwd_kernel(count_ref, rows_ref, cols_ref, bits_hbm, own_hbm, recv_hbm, tiles_hbm,
                     out_ref, token, tiles, src, acc, bits, sems):
    count = count_ref[0]
    own = pltpu.make_async_copy(own_hbm, src.at[pl.ds(0, RB)], sems.at[PIECES])
    got = pltpu.make_async_copy(recv_hbm, src.at[pl.ds(RB, 64)], sems.at[PIECES + 1])
    bits_in = pltpu.make_async_copy(bits_hbm, bits, sems.at[PIECES + 2])
    own.start()
    got.start()
    copies = tile_copies(tiles_hbm, tiles, sems)
    for c in copies:
        c.start()
    bits_in.start()
    acc[...] = jnp.zeros_like(acc)
    own.wait()
    got.wait()
    for k in range(PIECES):
        copies[k].wait()

        for t in range(k * PIECE, (k + 1) * PIECE):
            r = jnp.where(t < count, rows_ref[0, t], RB)
            acc[r] += dot(tiles[t], src[cols_ref[0, t]])

    token[...] = jnp.zeros_like(token)
    bits_in.wait()

    def mask(i, carry):
        at = pl.multiple_of(i * MASK_STEP, MASK_STEP)
        active = bit_mask(bits[:, pl.ds(at, MASK_STEP)])
        for j in range(MASK_STEP // B):
            b = i * (MASK_STEP // B) + j
            out_ref[b] = jnp.where(active[j * B : (j + 1) * B], acc[b], 0.0).astype(BF16)
        return carry

    lax.fori_loop(0, 4096 // MASK_STEP, mask, 0)


def tiles_fwd_call(count, rows, cols, bits_t, own, recv, tiles):
    return pl.pallas_call(
        tiles_fwd_kernel,
        out_shape=[jax.ShapeDtypeStruct((RB, B, B), BF16), jax.ShapeDtypeStruct((8, B), F32)],
        in_specs=[SMEM] * 3 + [ANY] * 4,
        out_specs=[VMEM] * 2,
        scratch_shapes=[
            pltpu.VMEM((TILES, B, B), BF16),
            pltpu.VMEM((RB + 64, B, B), BF16),
            pltpu.VMEM((RB + 1, B, B), F32),
            pltpu.VMEM((8, 4096), jnp.int32),
            pltpu.SemaphoreType.DMA((PIECES + 3,)),
        ],
        compiler_params=params(58),
        cost_estimate=cost(2 * TILES * B * B * B, 30 << 20),
        name="tiles_fwd",
    )(count, rows, cols, bits_t, own, recv, tiles)


def hidden_kernel(me_ref, send_ref, x0, x1, x2a, x2b, x3, w_ref, hid_hbm, out_hbm, hid, sems):
    me = me_ref[0]
    rhs = jnp.concatenate(
        [w_ref[pl.ds(pl.multiple_of(rel(me, -s) * B, B), B), :] for s in range(HID)], 0
    )
    for n in range(4096 // STEP):
        half, at = (x2a, n * STEP) if n < 2048 // STEP else (x2b, n * STEP - 2048)
        here = slice(n * STEP, (n + 1) * STEP)
        lhs = jnp.concatenate([x0[here, :], x1[here, :], half[at : at + STEP, :], x3[here, :]], 1)
        r = dot(lhs, rhs).astype(BF16)
        for j in range(STEP // B):
            hid[n * (STEP // B) + j] = r[j * B : (j + 1) * B]
    copies = [
        pltpu.make_async_copy(hid.at[send_ref[0, q]], out_hbm.at[q], sems.at[q]) for q in range(64)
    ]
    copies.append(pltpu.make_async_copy(hid, hid_hbm, sems.at[64]))
    for c in copies:
        c.start()
    for c in copies:
        c.wait()


def hidden_call(me, send, xs, w):
    return pl.pallas_call(
        hidden_kernel,
        out_shape=[
            jax.ShapeDtypeStruct((RB, B, B), BF16),
            jax.ShapeDtypeStruct((64, B, B), BF16),
        ],
        in_specs=[SMEM] * 2 + [VMEM] * 6,
        out_specs=[HBM] * 2,
        scratch_shapes=[pltpu.VMEM((RB, B, B), BF16), pltpu.SemaphoreType.DMA((65,))],
        compiler_params=params(),
        cost_estimate=cost(2 * 4096 * 512 * 128, 10 << 20),
        name="hidden",
    )(me, send, *xs, w)


def sum_kernel(me_ref, send_ref, own_hbm, got_hbm, x0, x1, x2a, x2b, x3, w_hbm, after,
               terms_hbm, p0, p1, p2a, p2b, p3, acc, got, xv, w, flat, pv, terms, sems, out_sems):
    me, y = me_ref[0], me_ref[1]
    ins = [
        pltpu.make_async_copy(own_hbm, acc, sems.at[0]),
        pltpu.make_async_copy(got_hbm, got, sems.at[1]),
        pltpu.make_async_copy(x0, xv.at[0], sems.at[2]),
        pltpu.make_async_copy(x1, xv.at[1], sems.at[3]),
        pltpu.make_async_copy(x2a, xv.at[2, pl.ds(0, 2048)], sems.at[4]),
        pltpu.make_async_copy(x2b, xv.at[2, pl.ds(2048, 2048)], sems.at[5]),
        pltpu.make_async_copy(x3, xv.at[3], sems.at[6]),
        pltpu.make_async_copy(w_hbm, w, sems.at[7]),
    ]
    for i in ins:
        i.start()
    ins[0].wait()
    ins[1].wait()

    def body(i, carry):
        for j in range(8):
            q = i * 8 + j
            acc[send_ref[0, q]] += got[q].astype(F32)
        return carry

    lax.fori_loop(0, 8, body, 0)
    outs = []

    ins[7].wait()
    rhs = jnp.concatenate(
        [w[pl.ds(pl.multiple_of(rel(me, s) * B, B), B), :] for s in range(HID)], 0
    )

    def part(i, carry):
        d = jnp.concatenate([acc[i * 4 + j].T.astype(BF16) for j in range(4)], 0)
        r = dot(d, rhs, ((1,), (1,))).astype(BF16)
        for s in range(HID):
            pv[s, pl.ds(pl.multiple_of(i * 512, 512), 512), :] = r[:, s * B : (s + 1) * B]
        return carry

    lax.fori_loop(0, RB // 4, part, 0)
    low, high = pl.ds(0, 2048), pl.ds(2048, 2048)
    for k, (p, v) in enumerate(
        ((p2a, pv.at[2, low]), (p2b, pv.at[2, high]), (p0, pv.at[0]), (p1, pv.at[1]), (p3, pv.at[3]))
    ):
        outs.append(pltpu.make_async_copy(v, p, out_sems.at[k]))
        outs[-1].start()
    for b in range(RB):
        flat[:, b * B : (b + 1) * B] = acc[b].astype(BF16)
    for i in ins[2:7]:
        i.wait()
    for s in range(HID):
        r = dot(flat[...], xv[s]).T
        terms[pl.ds(pl.multiple_of(rel(me, -s) * B, B), B), :] = r
    for k in range(4):
        at = pl.multiple_of(lax.rem(y + k, 4) * B, B)
        outs.append(
            pltpu.make_async_copy(
                terms.at[pl.ds(at, B)], terms_hbm.at[pl.ds(k * B, B)], out_sems.at[5 + k]
            )
        )
        outs[-1].start()
    for o in outs:
        o.wait()


def sum_call(me, send, own, got, xs, w, after):
    return pl.pallas_call(
        sum_kernel,
        out_shape=[jax.ShapeDtypeStruct((512, B), F32)]
        + [jax.ShapeDtypeStruct((n, B), BF16) for n in (4096, 4096, 2048, 2048, 4096)],
        in_specs=[SMEM] * 2 + [ANY] * 9,
        out_specs=[HBM] * 6,
        scratch_shapes=[
            pltpu.VMEM((RB, B, B), F32),
            pltpu.VMEM((64, B, B), BF16),
            pltpu.VMEM((HID, 4096, B), BF16),
            pltpu.VMEM((512, B), BF16),
            pltpu.VMEM((B, 4096), BF16),
            pltpu.VMEM((HID, 4096, B), BF16),
            pltpu.VMEM((512, B), F32),
            pltpu.SemaphoreType.DMA((8,)),
            pltpu.SemaphoreType.DMA((9,)),
        ],
        compiler_params=params(),
        cost_estimate=cost(2 * 4096 * 512 * 128, 12 << 20),
        name="sum_returned",
    )(me, send, own, got, *xs, w, after)


def add_kernel(a, b, c, d, out):
    out[...] = ((a[...] + b[...]) + (c[...] + d[...])).astype(BF16)


def add_call(parts):
    return pl.pallas_call(
        add_kernel,
        out_shape=jax.ShapeDtypeStruct((B, B), BF16),
        in_specs=[VMEM] * 4,
        out_specs=VMEM,
        compiler_params=params(8),
        cost_estimate=cost(4 * B * B, 1 << 18),
        name="add_y",
    )(*parts)


def add_z_kernel(me_ref, p0, p1, p2, p3, out, by_z):
    z = lax.div(me_ref[2], 2)
    for k, p in enumerate((p0, p1, p2, p3)):
        by_z[rel(z, -k)] = p[...].astype(F32)
    out[...] = (by_z[0] + by_z[1]) + (by_z[2] + by_z[3])


def add_z_call(me, parts):
    return pl.pallas_call(
        add_z_kernel,
        out_shape=jax.ShapeDtypeStruct((B, B), F32),
        in_specs=[SMEM] + [VMEM] * 4,
        out_specs=VMEM,
        scratch_shapes=[pltpu.VMEM((4, B, B), F32)],
        compiler_params=params(8),
        cost_estimate=cost(8 * B * B, 1 << 19),
        name="add_z",
    )(me, *parts)


def pair_kernel(a, b, after, out):
    out[...] = a[...] + b[...]


def pair_call(a, b, after):
    return pl.pallas_call(
        pair_kernel,
        out_shape=jax.ShapeDtypeStruct((B, B), F32),
        in_specs=[VMEM] * 2 + [ANY],
        out_specs=VMEM,
        compiler_params=params(8),
        cost_estimate=cost(B * B, 1 << 18),
        name="add_pair",
    )(a, b, after)


def relay_kernel(p1, p3, low, high, after, out1, out3):
    half = 2048
    out1[:half, :] = (p1[:half, :].astype(F32) + low[...].astype(F32)).astype(BF16)
    out1[half:, :] = p1[half:, :]
    out3[:half, :] = p3[:half, :]
    out3[half:, :] = (p3[half:, :].astype(F32) + high[...].astype(F32)).astype(BF16)


def relay_call(p1, p3, low, high, after):
    return pl.pallas_call(
        relay_kernel,
        out_shape=[jax.ShapeDtypeStruct((4096, B), BF16)] * 2,
        in_specs=[VMEM] * 4 + [ANY],
        out_specs=[VMEM] * 2,
        compiler_params=params(16),
        cost_estimate=cost(4096 * B, 6 << 20),
        name="relay",
    )(p1, p3, low, high, after)


def parts_kernel(p0, q1, q3, after, ig_hbm, p, ig, sems, out_sems):
    rows = [pl.ds(k * 1024, 1024) for k in range(4)]
    ins = [
        [pltpu.make_async_copy(v.at[r], p.at[s, r], sems.at[3 * k + s]) for s, v in enumerate((p0, q1, q3))]
        for k, r in enumerate(rows)
    ]
    for group in ins:
        for c in group:
            c.start()
    outs = []
    for k, r in enumerate(rows):
        for c in ins[k]:
            c.wait()
        v = p[0, r, :].astype(F32) + (p[1, r, :].astype(F32) + p[2, r, :].astype(F32))
        ig[r, :] = v.astype(BF16)
        outs.append(pltpu.make_async_copy(ig.at[r], ig_hbm.at[r], out_sems.at[k]))
        outs[-1].start()
    for c in outs:
        c.wait()


def parts_call(parts, after):
    return pl.pallas_call(
        parts_kernel,
        out_shape=jax.ShapeDtypeStruct((4096, B), BF16),
        in_specs=[ANY] * 4,
        out_specs=HBM,
        scratch_shapes=[
            pltpu.VMEM((3, 4096, B), BF16),
            pltpu.VMEM((4096, B), BF16),
            pltpu.SemaphoreType.DMA((12,)),
            pltpu.SemaphoreType.DMA((4,)),
        ],
        compiler_params=params(16),
        cost_estimate=cost(4096 * B * 4, 6 << 20),
        name="add_parts",
    )(*parts, after)


def finish_kernel(me_ref, t0, t1, t2, t3, out):
    for k, t in enumerate((t0, t1, t2, t3)):
        out[pl.ds(pl.multiple_of(rel(me_ref[1], -k) * B, B), B), :] = t[...]


def finish_call(me, totals):
    return pl.pallas_call(
        finish_kernel,
        out_shape=jax.ShapeDtypeStruct((512, B), F32),
        in_specs=[SMEM] + [VMEM] * 4,
        out_specs=VMEM,
        compiler_params=params(8),
        cost_estimate=cost(512 * B, 1 << 19),
        name="finish",
    )(me, *totals)


def shift_hid(v, s):
    return lax.ppermute(v, "hid", [(i, (i + s) % HID) for i in range(HID)])


def split_kernel(v1, v3, after, low, high):
    low[...] = v1[...]
    high[...] = v3[...]


def split_call(v1, v3, after):
    half = jax.ShapeDtypeStruct((2048, B), BF16)
    return pl.pallas_call(
        split_kernel,
        out_shape=[half] * 2,
        grid=(1,),
        in_specs=[
            pl.BlockSpec((2048, B), lambda i: (0, 0)),
            pl.BlockSpec((2048, B), lambda i: (1, 0)),
            ANY,
        ],
        out_specs=[pl.BlockSpec((2048, B), lambda i: (0, 0))] * 2,
        compiler_params=params(12),
        cost_estimate=cost(1000, 2 << 20),
        name="halves",
    )(v1, v3, after)


def gather_hid(v, after):
    v1, v3 = shift_hid(v, 1), shift_hid(v, 3)
    low, high = split_call(v1, v3, after)
    return v, v1, shift_hid(low, 1), shift_hid(high, 3), v3


def shift_dom(v, dz, dy, dc):
    pairs = [
        ((z * 4 + y) * 2 + c, (((z + dz) % 8) * 4 + (y + dy) % 4) * 2 + (c ^ dc))
        for z in range(8)
        for y in range(4)
        for c in range(2)
    ]
    return lax.ppermute(v, "dom", pairs)


def swap_z(v):
    return lax.ppermute(v, "dom", [(i, i ^ 8) for i in range(64)])


def all_to_all(v):
    return lax.all_to_all(v, "dom", split_axis=0, concat_axis=0, tiled=True)


def per_device(x, w, tiles, rows, cols, count, send, bits, cot):
    hid = lax.axis_index("hid").astype(jnp.int32)
    dom = lax.axis_index("dom").astype(jnp.int32)
    z, y = dom // 8, (dom // 2) % 4
    me = jnp.stack([hid, y, z])
    bits_t = bits.T

    own, slots = tiles_bwd_call(count, rows, cols, bits_t, cot, tiles)
    returned = all_to_all(slots)

    xs = gather_hid(x, slots)
    hidden, outgoing = hidden_call(me, send, xs, w)
    incoming = all_to_all(outgoing)

    terms, p0, p1, p2a, p2b, p3 = sum_call(me, send, own, returned, xs, w, outgoing)

    terms = (terms + shift_dom(terms, 0, 0, 1)).reshape(4, B, B)
    terms = [terms[0]] + [shift_dom(terms[k], 0, k, 0) for k in (1, 3, 2)]
    part = add_call(terms)

    p1, p3 = relay_call(p1, p3, shift_hid(p2a, 1), shift_hid(p2b, 3), part)
    parts = [p0, shift_hid(p1, 1), shift_hid(p3, 3)]

    total = add_z_call(me, [part] + [shift_dom(part, k, 0, 0) for k in (2, 4, 6)])
    out_act, token = tiles_fwd_call(count, rows, cols, bits_t, hidden, incoming, tiles)
    total = pair_call(total, swap_z(total), token)
    weight_grad = finish_call(me, [total] + [shift_dom(total, 0, k, 0) for k in range(1, 4)])
    input_grad = parts_call(parts, token)
    return out_act.reshape(4096, B), input_grad, weight_grad


def solution(mesh):
    placed = (
        P("dom", "hid"),
        P(None, "hid"),
        P("dom", None, None),
        P("dom", None),
        P("dom", None),
        P("dom"),
        P("dom", None),
        P("dom", "hid"),
        P("dom", "hid"),
    )
    return jax.shard_map(
        per_device,
        mesh=mesh,
        in_specs=placed,
        out_specs=(P("dom", "hid"), P("dom", "hid"), P(None, "hid")),
        check_vma=False,
    )
```

```python
import functools

import jax
import jax.numpy as jnp
from jax import lax
from jax.experimental import pallas as pl
from jax.experimental.pallas import tpu as pltpu
from jax.sharding import PartitionSpec as P

B = 128
RB = 32
HID = 4
CHUNK = RB // HID
F32 = jnp.float32
BF16 = jnp.bfloat16
MIB = 1024 * 1024

VMEM = pl.BlockSpec(memory_space=pltpu.VMEM)
SMEM = pl.BlockSpec(memory_space=pltpu.SMEM)
ANY = pl.BlockSpec(memory_space=pl.ANY)
HBM = pl.BlockSpec(memory_space=pltpu.HBM)


def params(mib=60):
    return pltpu.CompilerParams(vmem_limit_bytes=mib * MIB)


def cost(flops, nbytes):
    return pl.CostEstimate(flops=flops, bytes_accessed=nbytes, transcendentals=0)


def dot(a, b, dims=((1,), (0,))):
    return lax.dot_general(a, b, (dims, ((), ())), preferred_element_type=F32)


def rel(me, shift):
    return lax.rem(me + shift + HID, HID)


def bit_mask(words):
    halves = jnp.concatenate([words & 255, words >> 8], 0).astype(F32).astype(BF16)
    row = lax.broadcasted_iota(jnp.int32, (16, B), 0)
    unit = lax.broadcasted_iota(jnp.int32, (16, B), 1)
    byte_row = (unit // 16) + 8 * ((unit % 16) // 8)
    scale = lax.div(jnp.ones((16, B), F32), (1 << (unit % 8)).astype(F32))
    spread = jnp.where(row == byte_row, scale, 0.0).astype(BF16)
    shifted = dot(halves, spread, ((0,), (0,)))
    return (shifted.astype(jnp.int32) & 1) == 1


STEP = 256
MASK_STEP = 2048
TILES = 176
PIECES = 4
PIECE = TILES // PIECES


def tile_copies(tiles_hbm, tiles, sems):
    return [
        pltpu.make_async_copy(
            tiles_hbm.at[pl.ds(k * PIECE, PIECE)], tiles.at[pl.ds(k * PIECE, PIECE)], sems.at[k]
        )
        for k in range(PIECES)
    ]


def tiles_bwd_kernel(count_ref, rows_ref, cols_ref, bits_hbm, cot_hbm, tiles_hbm, own_hbm,
                     slot_hbm, tiles, bits, cot, d_t, acc, slots, sems, out_sems):
    count = count_ref[0]
    bits_in = pltpu.make_async_copy(bits_hbm, bits, sems.at[PIECES])
    steps = [pl.ds(i * MASK_STEP, MASK_STEP) for i in range(4096 // MASK_STEP)]
    cot_in = [
        pltpu.make_async_copy(cot_hbm.at[r], cot.at[r], sems.at[PIECES + 1 + i])
        for i, r in enumerate(steps)
    ]
    bits_in.start()
    for c in cot_in:
        c.start()
    copies = tile_copies(tiles_hbm, tiles, sems)
    for c in copies:
        c.start()
    acc[...] = jnp.zeros_like(acc)
    bits_in.wait()

    for i, r in enumerate(steps):
        cot_in[i].wait()
        active = bit_mask(bits[:, r])
        v = jnp.where(active, cot[r, :].astype(F32), 0.0)
        for j in range(MASK_STEP // B):
            d_t[i * (MASK_STEP // B) + j] = v[j * B : (j + 1) * B].T.astype(BF16)
    for k in range(PIECES):
        copies[k].wait()

        for t in range(k * PIECE, (k + 1) * PIECE):
            s = jnp.where(t < count, cols_ref[0, t], RB + 64)
            acc[s] += dot(d_t[rows_ref[0, t]], tiles[t])
    outs = [pltpu.make_async_copy(acc.at[pl.ds(0, RB)], own_hbm, out_sems.at[4])]
    outs[0].start()
    for k in range(4):
        at = pl.ds(k * 16, 16)
        slots[at] = acc[RB + k * 16 : RB + (k + 1) * 16].astype(BF16)
        outs.append(pltpu.make_async_copy(slots.at[at], slot_hbm.at[at], out_sems.at[k]))
        outs[-1].start()
    for c in outs:
        c.wait()


def tiles_bwd_call(count, rows, cols, bits_t, cot, tiles):
    return pl.pallas_call(
        tiles_bwd_kernel,
        out_shape=[
            jax.ShapeDtypeStruct((RB, B, B), F32),
            jax.ShapeDtypeStruct((64, B, B), BF16),
        ],
        in_specs=[SMEM] * 3 + [ANY] * 3,
        out_specs=[HBM] * 2,
        scratch_shapes=[
            pltpu.VMEM((TILES, B, B), BF16),
            pltpu.VMEM((8, 4096), jnp.int32),
            pltpu.VMEM((4096, B), BF16),
            pltpu.VMEM((RB, B, B), BF16),
            pltpu.VMEM((RB + 65, B, B), F32),
            pltpu.VMEM((64, B, B), BF16),
            pltpu.SemaphoreType.DMA((PIECES + 3,)),
            pltpu.SemaphoreType.DMA((5,)),
        ],
        compiler_params=params(),
        cost_estimate=cost(2 * TILES * B * B * B, 30 << 20),
        name="tiles_bwd",
    )(count, rows, cols, bits_t, cot, tiles)


def active_kernel(bits_ref, mask_ref, token):
    for i in range(4096 // MASK_STEP):
        r = pl.ds(i * MASK_STEP, MASK_STEP)
        mask_ref[r, :] = jnp.where(bit_mask(bits_ref[:, r]), 1.0, 0.0).astype(BF16)
    token[...] = jnp.zeros_like(token)


def active_call(bits_t):
    return pl.pallas_call(
        active_kernel,
        out_shape=[jax.ShapeDtypeStruct((4096, B), BF16), jax.ShapeDtypeStruct((8, B), F32)],
        in_specs=[VMEM],
        out_specs=[VMEM] * 2,
        compiler_params=params(40),
        cost_estimate=cost(4096 * B * 40, 2 << 20),
        name="active",
    )(bits_t)


def tiles_fwd_kernel(count_ref, rows_ref, cols_ref, mask_hbm, own_hbm, recv_hbm, tiles_hbm,
                     out_ref, token, tiles, src, acc, active, sems):
    count = count_ref[0]
    own = pltpu.make_async_copy(own_hbm, src.at[pl.ds(0, RB)], sems.at[PIECES])
    got = pltpu.make_async_copy(recv_hbm, src.at[pl.ds(RB, 64)], sems.at[PIECES + 1])
    mask_in = pltpu.make_async_copy(mask_hbm, active, sems.at[PIECES + 2])
    own.start()
    got.start()
    copies = tile_copies(tiles_hbm, tiles, sems)
    for c in copies:
        c.start()
    mask_in.start()
    acc[...] = jnp.zeros_like(acc)
    own.wait()
    got.wait()
    for k in range(PIECES):
        copies[k].wait()

        for t in range(k * PIECE, (k + 1) * PIECE):
            r = jnp.where(t < count, rows_ref[0, t], RB)
            acc[r] += dot(tiles[t], src[cols_ref[0, t]])

    token[...] = jnp.zeros_like(token)
    mask_in.wait()

    for b in range(RB):
        keep = active[b * B : (b + 1) * B, :].astype(F32) > 0.5
        out_ref[b] = jnp.where(keep, acc[b], 0.0).astype(BF16)


def tiles_fwd_call(count, rows, cols, mask, own, recv, tiles):
    return pl.pallas_call(
        tiles_fwd_kernel,
        out_shape=[jax.ShapeDtypeStruct((RB, B, B), BF16), jax.ShapeDtypeStruct((8, B), F32)],
        in_specs=[SMEM] * 3 + [ANY] * 4,
        out_specs=[VMEM] * 2,
        scratch_shapes=[
            pltpu.VMEM((TILES, B, B), BF16),
            pltpu.VMEM((RB + 64, B, B), BF16),
            pltpu.VMEM((RB + 1, B, B), F32),
            pltpu.VMEM((4096, B), BF16),
            pltpu.SemaphoreType.DMA((PIECES + 3,)),
        ],
        compiler_params=params(58),
        cost_estimate=cost(2 * TILES * B * B * B, 30 << 20),
        name="tiles_fwd",
    )(count, rows, cols, mask, own, recv, tiles)


def hidden_kernel(me_ref, send_ref, x0, x1, x2a, x2b, x3, w_ref, after, hid_hbm, out_hbm, hid, sems):
    me = me_ref[0]
    rhs = jnp.concatenate(
        [w_ref[pl.ds(pl.multiple_of(rel(me, -s) * B, B), B), :] for s in range(HID)], 0
    )
    for n in range(4096 // STEP):
        half, at = (x2a, n * STEP) if n < 2048 // STEP else (x2b, n * STEP - 2048)
        here = slice(n * STEP, (n + 1) * STEP)
        lhs = jnp.concatenate([x0[here, :], x1[here, :], half[at : at + STEP, :], x3[here, :]], 1)
        r = dot(lhs, rhs).astype(BF16)
        for j in range(STEP // B):
            hid[n * (STEP // B) + j] = r[j * B : (j + 1) * B]
    copies = [
        pltpu.make_async_copy(hid.at[send_ref[0, q]], out_hbm.at[q], sems.at[q]) for q in range(64)
    ]
    copies.append(pltpu.make_async_copy(hid, hid_hbm, sems.at[64]))
    for c in copies:
        c.start()
    for c in copies:
        c.wait()


def hidden_call(me, send, xs, w, after):
    return pl.pallas_call(
        hidden_kernel,
        out_shape=[
            jax.ShapeDtypeStruct((RB, B, B), BF16),
            jax.ShapeDtypeStruct((64, B, B), BF16),
        ],
        in_specs=[SMEM] * 2 + [VMEM] * 6 + [ANY],
        out_specs=[HBM] * 2,
        scratch_shapes=[pltpu.VMEM((RB, B, B), BF16), pltpu.SemaphoreType.DMA((65,))],
        compiler_params=params(),
        cost_estimate=cost(2 * 4096 * 512 * 128, 10 << 20),
        name="hidden",
    )(me, send, *xs, w, after)


def sum_kernel(me_ref, send_ref, own_hbm, got_hbm, x0, x1, x2a, x2b, x3, w_hbm, after,
               terms_hbm, p0, p1, p2a, p2b, p3, acc, got, xv, w, flat, pv, terms, sems, out_sems):
    me, y = me_ref[0], me_ref[1]
    ins = [
        pltpu.make_async_copy(own_hbm, acc, sems.at[0]),
        pltpu.make_async_copy(got_hbm, got, sems.at[1]),
        pltpu.make_async_copy(x0, xv.at[0], sems.at[2]),
        pltpu.make_async_copy(x1, xv.at[1], sems.at[3]),
        pltpu.make_async_copy(x2a, xv.at[2, pl.ds(0, 2048)], sems.at[4]),
        pltpu.make_async_copy(x2b, xv.at[2, pl.ds(2048, 2048)], sems.at[5]),
        pltpu.make_async_copy(x3, xv.at[3], sems.at[6]),
        pltpu.make_async_copy(w_hbm, w, sems.at[7]),
    ]
    for i in ins:
        i.start()
    ins[0].wait()
    ins[1].wait()

    def body(i, carry):
        for j in range(8):
            q = i * 8 + j
            acc[send_ref[0, q]] += got[q].astype(F32)
        return carry

    lax.fori_loop(0, 8, body, 0)
    outs = []

    ins[7].wait()
    rhs = jnp.concatenate(
        [w[pl.ds(pl.multiple_of(rel(me, s) * B, B), B), :] for s in range(HID)], 0
    )

    def part(i, carry):
        d = jnp.concatenate([acc[i * 4 + j].T.astype(BF16) for j in range(4)], 0)
        r = dot(d, rhs, ((1,), (1,))).astype(BF16)
        for s in range(HID):
            pv[s, pl.ds(pl.multiple_of(i * 512, 512), 512), :] = r[:, s * B : (s + 1) * B]
        return carry

    lax.fori_loop(0, RB // 4, part, 0)
    low, high = pl.ds(0, 2048), pl.ds(2048, 2048)
    for k, (p, v) in enumerate(
        ((p2a, pv.at[2, low]), (p2b, pv.at[2, high]), (p0, pv.at[0]), (p1, pv.at[1]), (p3, pv.at[3]))
    ):
        outs.append(pltpu.make_async_copy(v, p, out_sems.at[k]))
        outs[-1].start()
    for b in range(RB):
        flat[:, b * B : (b + 1) * B] = acc[b].astype(BF16)
    for i in ins[2:7]:
        i.wait()
    for s in range(HID):
        r = dot(flat[...], xv[s]).T
        terms[pl.ds(pl.multiple_of(rel(me, -s) * B, B), B), :] = r
    for k in range(4):
        at = pl.multiple_of(lax.rem(y + k, 4) * B, B)
        outs.append(
            pltpu.make_async_copy(
                terms.at[pl.ds(at, B)], terms_hbm.at[pl.ds(k * B, B)], out_sems.at[5 + k]
            )
        )
        outs[-1].start()
    for o in outs:
        o.wait()


def sum_call(me, send, own, got, xs, w, after):
    return pl.pallas_call(
        sum_kernel,
        out_shape=[jax.ShapeDtypeStruct((512, B), F32)]
        + [jax.ShapeDtypeStruct((n, B), BF16) for n in (4096, 4096, 2048, 2048, 4096)],
        in_specs=[SMEM] * 2 + [ANY] * 9,
        out_specs=[HBM] * 6,
        scratch_shapes=[
            pltpu.VMEM((RB, B, B), F32),
            pltpu.VMEM((64, B, B), BF16),
            pltpu.VMEM((HID, 4096, B), BF16),
            pltpu.VMEM((512, B), BF16),
            pltpu.VMEM((B, 4096), BF16),
            pltpu.VMEM((HID, 4096, B), BF16),
            pltpu.VMEM((512, B), F32),
            pltpu.SemaphoreType.DMA((8,)),
            pltpu.SemaphoreType.DMA((9,)),
        ],
        compiler_params=params(),
        cost_estimate=cost(2 * 4096 * 512 * 128, 12 << 20),
        name="sum_returned",
    )(me, send, own, got, *xs, w, after)


def add_kernel(a, b, c, d, out):
    out[...] = ((a[...] + b[...]) + (c[...] + d[...])).astype(BF16)


def add_call(parts):
    return pl.pallas_call(
        add_kernel,
        out_shape=jax.ShapeDtypeStruct((B, B), BF16),
        in_specs=[VMEM] * 4,
        out_specs=VMEM,
        compiler_params=params(8),
        cost_estimate=cost(4 * B * B, 1 << 18),
        name="add_y",
    )(*parts)


def add_z_kernel(me_ref, p0, p1, p2, p3, out, by_z):
    z = me_ref[2] & 3
    for k, p in enumerate((p0, p1, p2, p3)):
        by_z[z ^ k] = p[...].astype(F32)
    out[...] = ((by_z[0] + by_z[1]) + (by_z[2] + by_z[3])).astype(BF16)


def add_z_call(me, parts):
    return pl.pallas_call(
        add_z_kernel,
        out_shape=jax.ShapeDtypeStruct((B, B), BF16),
        in_specs=[SMEM] + [VMEM] * 4,
        out_specs=VMEM,
        scratch_shapes=[pltpu.VMEM((4, B, B), F32)],
        compiler_params=params(8),
        cost_estimate=cost(8 * B * B, 1 << 19),
        name="add_z",
    )(me, *parts)


def pair_kernel(a, b, after, out):
    out[...] = a[...].astype(F32) + b[...].astype(F32)


def pair_call(a, b, after):
    return pl.pallas_call(
        pair_kernel,
        out_shape=jax.ShapeDtypeStruct((B, B), F32),
        in_specs=[VMEM] * 2 + [ANY],
        out_specs=VMEM,
        compiler_params=params(8),
        cost_estimate=cost(B * B, 1 << 18),
        name="add_pair",
    )(a, b, after)


def relay_kernel(p1, p3, low, high, after, out1, out3):
    half = 2048
    out1[:half, :] = (p1[:half, :].astype(F32) + low[...].astype(F32)).astype(BF16)
    out1[half:, :] = p1[half:, :]
    out3[:half, :] = p3[:half, :]
    out3[half:, :] = (p3[half:, :].astype(F32) + high[...].astype(F32)).astype(BF16)


def relay_call(p1, p3, low, high, after):
    return pl.pallas_call(
        relay_kernel,
        out_shape=[jax.ShapeDtypeStruct((4096, B), BF16)] * 2,
        in_specs=[VMEM] * 4 + [ANY],
        out_specs=[VMEM] * 2,
        compiler_params=params(16),
        cost_estimate=cost(4096 * B, 6 << 20),
        name="relay",
    )(p1, p3, low, high, after)


def parts_kernel(p0, q1, q3, after, ig_hbm, p, ig, sems, out_sems):
    rows = [pl.ds(k * 1024, 1024) for k in range(4)]
    ins = [
        [pltpu.make_async_copy(v.at[r], p.at[s, r], sems.at[3 * k + s]) for s, v in enumerate((p0, q1, q3))]
        for k, r in enumerate(rows)
    ]
    for group in ins:
        for c in group:
            c.start()
    outs = []
    for k, r in enumerate(rows):
        for c in ins[k]:
            c.wait()
        v = p[0, r, :].astype(F32) + (p[1, r, :].astype(F32) + p[2, r, :].astype(F32))
        ig[r, :] = v.astype(BF16)
        outs.append(pltpu.make_async_copy(ig.at[r], ig_hbm.at[r], out_sems.at[k]))
        outs[-1].start()
    for c in outs:
        c.wait()


def parts_call(parts, after):
    return pl.pallas_call(
        parts_kernel,
        out_shape=jax.ShapeDtypeStruct((4096, B), BF16),
        in_specs=[ANY] * 4,
        out_specs=HBM,
        scratch_shapes=[
            pltpu.VMEM((3, 4096, B), BF16),
            pltpu.VMEM((4096, B), BF16),
            pltpu.SemaphoreType.DMA((12,)),
            pltpu.SemaphoreType.DMA((4,)),
        ],
        compiler_params=params(16),
        cost_estimate=cost(4096 * B * 4, 6 << 20),
        name="add_parts",
    )(*parts, after)


def finish_kernel(me_ref, t0, t1, t2, t3, out):
    for k, t in enumerate((t0, t1, t2, t3)):
        out[pl.ds(pl.multiple_of(rel(me_ref[1], -k) * B, B), B), :] = t[...]


def finish_call(me, totals):
    return pl.pallas_call(
        finish_kernel,
        out_shape=jax.ShapeDtypeStruct((512, B), F32),
        in_specs=[SMEM] + [VMEM] * 4,
        out_specs=VMEM,
        compiler_params=params(8),
        cost_estimate=cost(512 * B, 1 << 19),
        name="finish",
    )(me, *totals)


def shift_hid(v, s):
    return lax.ppermute(v, "hid", [(i, (i + s) % HID) for i in range(HID)])


def split_kernel(v1, v3, after, low, high):
    low[...] = v1[...]
    high[...] = v3[...]


def split_call(v1, v3, after):
    half = jax.ShapeDtypeStruct((2048, B), BF16)
    return pl.pallas_call(
        split_kernel,
        out_shape=[half] * 2,
        grid=(1,),
        in_specs=[
            pl.BlockSpec((2048, B), lambda i: (0, 0)),
            pl.BlockSpec((2048, B), lambda i: (1, 0)),
            ANY,
        ],
        out_specs=[pl.BlockSpec((2048, B), lambda i: (0, 0))] * 2,
        compiler_params=params(12),
        cost_estimate=cost(1000, 2 << 20),
        name="halves",
    )(v1, v3, after)


def gather_hid(v, after):
    v1, v3 = shift_hid(v, 1), shift_hid(v, 3)
    low, high = split_call(v1, v3, after)
    return v, v1, shift_hid(low, 1), shift_hid(high, 3), v3


def shift_dom(v, dz, dy, dc):
    pairs = [
        ((z * 4 + y) * 2 + c, (((z + dz) % 8) * 4 + (y + dy) % 4) * 2 + (c ^ dc))
        for z in range(8)
        for y in range(4)
        for c in range(2)
    ]
    return lax.ppermute(v, "dom", pairs)


def swap_z(v, k):
    return lax.ppermute(v, "dom", [(i, i ^ (8 * k)) for i in range(64)])


def all_to_all(v):
    return lax.all_to_all(v, "dom", split_axis=0, concat_axis=0, tiled=True)


def per_device(x, w, tiles, rows, cols, count, send, bits, cot):
    hid = lax.axis_index("hid").astype(jnp.int32)
    dom = lax.axis_index("dom").astype(jnp.int32)
    z, y = dom // 8, (dom // 2) % 4
    me = jnp.stack([hid, y, z])
    bits_t = bits.T

    own, slots = tiles_bwd_call(count, rows, cols, bits_t, cot, tiles)
    returned = all_to_all(slots)

    xs = gather_hid(x, slots)
    mask, ready = active_call(bits_t)
    hidden, outgoing = hidden_call(me, send, xs, w, ready)
    incoming = all_to_all(outgoing)

    terms, p0, p1, p2a, p2b, p3 = sum_call(me, send, own, returned, xs, w, outgoing)

    terms = (terms + shift_dom(terms, 0, 0, 1)).reshape(4, B, B)
    terms = [terms[0]] + [shift_dom(terms[k], 0, k, 0) for k in (1, 3, 2)]
    part = add_call(terms)

    p1, p3 = relay_call(p1, p3, shift_hid(p2a, 1), shift_hid(p2b, 3), part)
    parts = [p0, shift_hid(p1, 1), shift_hid(p3, 3)]

    total = add_z_call(me, [part] + [swap_z(part, k) for k in (1, 2, 3)])
    out_act, token = tiles_fwd_call(count, rows, cols, mask, hidden, incoming, tiles)
    total = pair_call(total, swap_z(total, 4), token)
    weight_grad = finish_call(me, [total] + [shift_dom(total, 0, k, 0) for k in range(1, 4)])
    input_grad = parts_call(parts, token)
    return out_act.reshape(4096, B), input_grad, weight_grad


def solution(mesh):
    placed = (
        P("dom", "hid"),
        P(None, "hid"),
        P("dom", None, None),
        P("dom", None),
        P("dom", None),
        P("dom"),
        P("dom", None),
        P("dom", "hid"),
        P("dom", "hid"),
    )
    return jax.shard_map(
        per_device,
        mesh=mesh,
        in_specs=placed,
        out_specs=(P("dom", "hid"), P("dom", "hid"), P(None, "hid")),
        check_vma=False,
    )
```

```python
import functools

import jax
import jax.numpy as jnp
from jax import lax
from jax.experimental import pallas as pl
from jax.experimental.pallas import tpu as pltpu
from jax.sharding import PartitionSpec as P

B = 128
RB = 32
HID = 4
CHUNK = RB // HID
F32 = jnp.float32
BF16 = jnp.bfloat16
MIB = 1024 * 1024

VMEM = pl.BlockSpec(memory_space=pltpu.VMEM)
SMEM = pl.BlockSpec(memory_space=pltpu.SMEM)
ANY = pl.BlockSpec(memory_space=pl.ANY)
HBM = pl.BlockSpec(memory_space=pltpu.HBM)


def params(mib=60):
    return pltpu.CompilerParams(vmem_limit_bytes=mib * MIB)


def cost(flops, nbytes):
    return pl.CostEstimate(flops=flops, bytes_accessed=nbytes, transcendentals=0)


def dot(a, b, dims=((1,), (0,))):
    return lax.dot_general(a, b, (dims, ((), ())), preferred_element_type=F32)


def rel(me, shift):
    return lax.rem(me + shift + HID, HID)


def bit_mask(words):
    halves = jnp.concatenate([words & 255, words >> 8], 0).astype(F32).astype(BF16)
    row = lax.broadcasted_iota(jnp.int32, (16, B), 0)
    unit = lax.broadcasted_iota(jnp.int32, (16, B), 1)
    byte_row = (unit // 16) + 8 * ((unit % 16) // 8)
    scale = lax.div(jnp.ones((16, B), F32), (1 << (unit % 8)).astype(F32))
    spread = jnp.where(row == byte_row, scale, 0.0).astype(BF16)
    shifted = dot(halves, spread, ((0,), (0,)))
    return (shifted.astype(jnp.int32) & 1) == 1


STEP = 256
MASK_STEP = 2048
TILES = 176
PIECES = 4
BACK_PIECES = 2


def tile_copies(tiles_hbm, tiles, sems, pieces):
    size = TILES // pieces
    return [
        pltpu.make_async_copy(
            tiles_hbm.at[pl.ds(k * size, size)], tiles.at[pl.ds(k * size, size)], sems.at[k]
        )
        for k in range(pieces)
    ]


def tiles_bwd_kernel(count_ref, rows_ref, cols_ref, bits_hbm, cot_hbm, tiles_hbm, own_hbm,
                     slot_hbm, tiles, bits, cot, d_t, acc, slots, sems, out_sems):
    count = count_ref[0]
    bits_in = pltpu.make_async_copy(bits_hbm, bits, sems.at[BACK_PIECES])
    steps = [pl.ds(i * MASK_STEP, MASK_STEP) for i in range(4096 // MASK_STEP)]
    cot_in = [
        pltpu.make_async_copy(cot_hbm.at[r], cot.at[r], sems.at[BACK_PIECES + 1 + i])
        for i, r in enumerate(steps)
    ]
    bits_in.start()
    for c in cot_in:
        c.start()
    copies = tile_copies(tiles_hbm, tiles, sems, BACK_PIECES)
    for c in copies:
        c.start()
    acc[...] = jnp.zeros_like(acc)
    bits_in.wait()

    for i, r in enumerate(steps):
        cot_in[i].wait()
        active = bit_mask(bits[:, r])
        v = jnp.where(active, cot[r, :].astype(F32), 0.0)
        for j in range(MASK_STEP // B):
            d_t[i * (MASK_STEP // B) + j] = v[j * B : (j + 1) * B].T.astype(BF16)
    for k in range(BACK_PIECES):
        copies[k].wait()

        for t in range(k * TILES // BACK_PIECES, (k + 1) * TILES // BACK_PIECES):
            s = jnp.where(t < count, cols_ref[0, t], RB + 64)
            acc[s] += dot(d_t[rows_ref[0, t]], tiles[t])
    outs = [pltpu.make_async_copy(acc.at[pl.ds(0, RB)], own_hbm, out_sems.at[4])]
    outs[0].start()
    for k in range(4):
        at = pl.ds(k * 16, 16)
        slots[at] = acc[RB + k * 16 : RB + (k + 1) * 16].astype(BF16)
        outs.append(pltpu.make_async_copy(slots.at[at], slot_hbm.at[at], out_sems.at[k]))
        outs[-1].start()
    for c in outs:
        c.wait()


def tiles_bwd_call(count, rows, cols, bits_t, cot, tiles):
    return pl.pallas_call(
        tiles_bwd_kernel,
        out_shape=[
            jax.ShapeDtypeStruct((RB, B, B), F32),
            jax.ShapeDtypeStruct((64, B, B), BF16),
        ],
        in_specs=[SMEM] * 3 + [ANY] * 3,
        out_specs=[HBM] * 2,
        scratch_shapes=[
            pltpu.VMEM((TILES, B, B), BF16),
            pltpu.VMEM((8, 4096), jnp.int32),
            pltpu.VMEM((4096, B), BF16),
            pltpu.VMEM((RB, B, B), BF16),
            pltpu.VMEM((RB + 65, B, B), F32),
            pltpu.VMEM((64, B, B), BF16),
            pltpu.SemaphoreType.DMA((BACK_PIECES + 3,)),
            pltpu.SemaphoreType.DMA((5,)),
        ],
        compiler_params=params(),
        cost_estimate=cost(2 * TILES * B * B * B, 30 << 20),
        name="tiles_bwd",
    )(count, rows, cols, bits_t, cot, tiles)


def active_kernel(bits_ref, mask_ref, token):
    for i in range(4096 // MASK_STEP):
        r = pl.ds(i * MASK_STEP, MASK_STEP)
        mask_ref[r, :] = jnp.where(bit_mask(bits_ref[:, r]), 1.0, 0.0).astype(BF16)
    token[...] = jnp.zeros_like(token)


def active_call(bits_t):
    return pl.pallas_call(
        active_kernel,
        out_shape=[jax.ShapeDtypeStruct((4096, B), BF16), jax.ShapeDtypeStruct((8, B), F32)],
        in_specs=[VMEM],
        out_specs=[VMEM] * 2,
        compiler_params=params(40),
        cost_estimate=cost(4096 * B * 40, 2 << 20),
        name="active",
    )(bits_t)


def tiles_fwd_kernel(count_ref, rows_ref, cols_ref, mask_hbm, own_hbm, recv_hbm, tiles_hbm,
                     out_hbm, token, tiles, src, acc, active, out, sems, out_sems):
    count = count_ref[0]
    own = pltpu.make_async_copy(own_hbm, src.at[pl.ds(0, RB)], sems.at[PIECES])
    got = pltpu.make_async_copy(recv_hbm, src.at[pl.ds(RB, 64)], sems.at[PIECES + 1])
    mask_in = pltpu.make_async_copy(mask_hbm, active, sems.at[PIECES + 2])
    own.start()
    got.start()
    copies = tile_copies(tiles_hbm, tiles, sems, PIECES)
    for c in copies:
        c.start()
    mask_in.start()
    acc[...] = jnp.zeros_like(acc)
    own.wait()
    got.wait()
    for k in range(PIECES):
        copies[k].wait()

        for t in range(k * TILES // PIECES, (k + 1) * TILES // PIECES):
            r = jnp.where(t < count, rows_ref[0, t], RB)
            acc[r] += dot(tiles[t], src[cols_ref[0, t]])

    token[...] = jnp.zeros_like(token)
    mask_in.wait()

    outs = []
    for k in range(4):
        at = pl.ds(k * CHUNK, CHUNK)
        for b in range(k * CHUNK, (k + 1) * CHUNK):
            keep = active[b * B : (b + 1) * B, :].astype(F32) > 0.5
            out[b] = jnp.where(keep, acc[b], 0.0).astype(BF16)
        outs.append(pltpu.make_async_copy(out.at[at], out_hbm.at[at], out_sems.at[k]))
        outs[-1].start()
    for c in outs:
        c.wait()


def tiles_fwd_call(count, rows, cols, mask, own, recv, tiles):
    return pl.pallas_call(
        tiles_fwd_kernel,
        out_shape=[jax.ShapeDtypeStruct((RB, B, B), BF16), jax.ShapeDtypeStruct((8, B), F32)],
        in_specs=[SMEM] * 3 + [ANY] * 4,
        out_specs=[HBM, VMEM],
        scratch_shapes=[
            pltpu.VMEM((TILES, B, B), BF16),
            pltpu.VMEM((RB + 64, B, B), BF16),
            pltpu.VMEM((RB + 1, B, B), F32),
            pltpu.VMEM((4096, B), BF16),
            pltpu.VMEM((RB, B, B), BF16),
            pltpu.SemaphoreType.DMA((PIECES + 3,)),
            pltpu.SemaphoreType.DMA((4,)),
        ],
        compiler_params=params(58),
        cost_estimate=cost(2 * TILES * B * B * B, 30 << 20),
        name="tiles_fwd",
    )(count, rows, cols, mask, own, recv, tiles)


def hidden_kernel(me_ref, send_ref, x0, x1, x2a, x2b, x3, w_ref, after, hid_hbm, out_hbm, hid, sems):
    me = me_ref[0]
    rhs = jnp.concatenate(
        [w_ref[pl.ds(pl.multiple_of(rel(me, -s) * B, B), B), :] for s in range(HID)], 0
    )
    for n in range(4096 // STEP):
        half, at = (x2a, n * STEP) if n < 2048 // STEP else (x2b, n * STEP - 2048)
        here = slice(n * STEP, (n + 1) * STEP)
        lhs = jnp.concatenate([x0[here, :], x1[here, :], half[at : at + STEP, :], x3[here, :]], 1)
        r = dot(lhs, rhs).astype(BF16)
        for j in range(STEP // B):
            hid[n * (STEP // B) + j] = r[j * B : (j + 1) * B]
    copies = [
        pltpu.make_async_copy(hid.at[send_ref[0, q]], out_hbm.at[q], sems.at[q]) for q in range(64)
    ]
    copies.append(pltpu.make_async_copy(hid, hid_hbm, sems.at[64]))
    for c in copies:
        c.start()
    for c in copies:
        c.wait()


def hidden_call(me, send, xs, w, after):
    return pl.pallas_call(
        hidden_kernel,
        out_shape=[
            jax.ShapeDtypeStruct((RB, B, B), BF16),
            jax.ShapeDtypeStruct((64, B, B), BF16),
        ],
        in_specs=[SMEM] * 2 + [VMEM] * 6 + [ANY],
        out_specs=[HBM] * 2,
        scratch_shapes=[pltpu.VMEM((RB, B, B), BF16), pltpu.SemaphoreType.DMA((65,))],
        compiler_params=params(),
        cost_estimate=cost(2 * 4096 * 512 * 128, 10 << 20),
        name="hidden",
    )(me, send, *xs, w, after)


def sum_kernel(me_ref, send_ref, own_hbm, got_hbm, x0, x1, x2a, x2b, x3, w_hbm, after,
               terms_hbm, p0, p1, p2a, p2b, p3, acc, got, xv, w, flat, pv, terms, sems, out_sems):
    me, y = me_ref[0], me_ref[1]
    ins = [
        pltpu.make_async_copy(own_hbm, acc, sems.at[0]),
        pltpu.make_async_copy(got_hbm, got, sems.at[1]),
        pltpu.make_async_copy(x0, xv.at[0], sems.at[2]),
        pltpu.make_async_copy(x1, xv.at[1], sems.at[3]),
        pltpu.make_async_copy(x2a, xv.at[2, pl.ds(0, 2048)], sems.at[4]),
        pltpu.make_async_copy(x2b, xv.at[2, pl.ds(2048, 2048)], sems.at[5]),
        pltpu.make_async_copy(x3, xv.at[3], sems.at[6]),
        pltpu.make_async_copy(w_hbm, w, sems.at[7]),
    ]
    for i in ins:
        i.start()
    ins[0].wait()
    ins[1].wait()

    def body(i, carry):
        for j in range(8):
            q = i * 8 + j
            acc[send_ref[0, q]] += got[q].astype(F32)
        return carry

    lax.fori_loop(0, 8, body, 0)
    outs = []

    ins[7].wait()
    rhs = jnp.concatenate(
        [w[pl.ds(pl.multiple_of(rel(me, s) * B, B), B), :] for s in range(HID)], 0
    )

    def part(i, carry):
        d = jnp.concatenate([acc[i * 4 + j].T.astype(BF16) for j in range(4)], 0)
        r = dot(d, rhs, ((1,), (1,))).astype(BF16)
        for s in range(HID):
            pv[s, pl.ds(pl.multiple_of(i * 512, 512), 512), :] = r[:, s * B : (s + 1) * B]
        return carry

    lax.fori_loop(0, RB // 4, part, 0)
    low, high = pl.ds(0, 2048), pl.ds(2048, 2048)
    for k, (p, v) in enumerate(
        ((p2a, pv.at[2, low]), (p2b, pv.at[2, high]), (p0, pv.at[0]), (p1, pv.at[1]), (p3, pv.at[3]))
    ):
        outs.append(pltpu.make_async_copy(v, p, out_sems.at[k]))
        outs[-1].start()
    for b in range(RB):
        flat[:, b * B : (b + 1) * B] = acc[b].astype(BF16)
    for i in ins[2:7]:
        i.wait()
    for s in range(HID):
        r = dot(flat[...], xv[s]).T
        terms[pl.ds(pl.multiple_of(rel(me, -s) * B, B), B), :] = r
    for k in range(4):
        at = pl.multiple_of(lax.rem(y + k, 4) * B, B)
        outs.append(
            pltpu.make_async_copy(
                terms.at[pl.ds(at, B)], terms_hbm.at[pl.ds(k * B, B)], out_sems.at[5 + k]
            )
        )
        outs[-1].start()
    for o in outs:
        o.wait()


def sum_call(me, send, own, got, xs, w, after):
    return pl.pallas_call(
        sum_kernel,
        out_shape=[jax.ShapeDtypeStruct((512, B), F32)]
        + [jax.ShapeDtypeStruct((n, B), BF16) for n in (4096, 4096, 2048, 2048, 4096)],
        in_specs=[SMEM] * 2 + [ANY] * 9,
        out_specs=[HBM] * 6,
        scratch_shapes=[
            pltpu.VMEM((RB, B, B), F32),
            pltpu.VMEM((64, B, B), BF16),
            pltpu.VMEM((HID, 4096, B), BF16),
            pltpu.VMEM((512, B), BF16),
            pltpu.VMEM((B, 4096), BF16),
            pltpu.VMEM((HID, 4096, B), BF16),
            pltpu.VMEM((512, B), F32),
            pltpu.SemaphoreType.DMA((8,)),
            pltpu.SemaphoreType.DMA((9,)),
        ],
        compiler_params=params(),
        cost_estimate=cost(2 * 4096 * 512 * 128, 12 << 20),
        name="sum_returned",
    )(me, send, own, got, *xs, w, after)


def add_kernel(a, b, c, d, out):
    out[...] = ((a[...] + b[...]) + (c[...] + d[...])).astype(BF16)


def add_call(parts):
    return pl.pallas_call(
        add_kernel,
        out_shape=jax.ShapeDtypeStruct((B, B), BF16),
        in_specs=[VMEM] * 4,
        out_specs=VMEM,
        compiler_params=params(8),
        cost_estimate=cost(4 * B * B, 1 << 18),
        name="add_y",
    )(*parts)


def add_z_kernel(me_ref, p0, p1, p2, p3, out, by_z):
    z = me_ref[2] & 3
    for k, p in enumerate((p0, p1, p2, p3)):
        by_z[z ^ k] = p[...].astype(F32)
    out[...] = ((by_z[0] + by_z[1]) + (by_z[2] + by_z[3])).astype(BF16)


def add_z_call(me, parts):
    return pl.pallas_call(
        add_z_kernel,
        out_shape=jax.ShapeDtypeStruct((B, B), BF16),
        in_specs=[SMEM] + [VMEM] * 4,
        out_specs=VMEM,
        scratch_shapes=[pltpu.VMEM((4, B, B), F32)],
        compiler_params=params(8),
        cost_estimate=cost(8 * B * B, 1 << 19),
        name="add_z",
    )(me, *parts)


def pair_kernel(a, b, after, out):
    out[...] = a[...].astype(F32) + b[...].astype(F32)


def pair_call(a, b, after):
    return pl.pallas_call(
        pair_kernel,
        out_shape=jax.ShapeDtypeStruct((B, B), F32),
        in_specs=[VMEM] * 2 + [ANY],
        out_specs=VMEM,
        compiler_params=params(8),
        cost_estimate=cost(B * B, 1 << 18),
        name="add_pair",
    )(a, b, after)


def relay_kernel(p1, p3, low, high, after, out1, out3):
    half = 2048
    out1[:half, :] = (p1[:half, :].astype(F32) + low[...].astype(F32)).astype(BF16)
    out1[half:, :] = p1[half:, :]
    out3[:half, :] = p3[:half, :]
    out3[half:, :] = (p3[half:, :].astype(F32) + high[...].astype(F32)).astype(BF16)


def relay_call(p1, p3, low, high, after):
    return pl.pallas_call(
        relay_kernel,
        out_shape=[jax.ShapeDtypeStruct((4096, B), BF16)] * 2,
        in_specs=[VMEM] * 4 + [ANY],
        out_specs=[VMEM] * 2,
        compiler_params=params(16),
        cost_estimate=cost(4096 * B, 6 << 20),
        name="relay",
    )(p1, p3, low, high, after)


def parts_kernel(p0, q1, q3, after, ig_hbm, p, ig, sems, out_sems):
    rows = [pl.ds(k * 1024, 1024) for k in range(4)]
    ins = [
        [pltpu.make_async_copy(v.at[r], p.at[s, r], sems.at[3 * k + s]) for s, v in enumerate((p0, q1, q3))]
        for k, r in enumerate(rows)
    ]
    for group in ins:
        for c in group:
            c.start()
    outs = []
    for k, r in enumerate(rows):
        for c in ins[k]:
            c.wait()
        v = p[0, r, :].astype(F32) + (p[1, r, :].astype(F32) + p[2, r, :].astype(F32))
        ig[r, :] = v.astype(BF16)
        outs.append(pltpu.make_async_copy(ig.at[r], ig_hbm.at[r], out_sems.at[k]))
        outs[-1].start()
    for c in outs:
        c.wait()


def parts_call(parts, after):
    return pl.pallas_call(
        parts_kernel,
        out_shape=jax.ShapeDtypeStruct((4096, B), BF16),
        in_specs=[ANY] * 4,
        out_specs=HBM,
        scratch_shapes=[
            pltpu.VMEM((3, 4096, B), BF16),
            pltpu.VMEM((4096, B), BF16),
            pltpu.SemaphoreType.DMA((12,)),
            pltpu.SemaphoreType.DMA((4,)),
        ],
        compiler_params=params(16),
        cost_estimate=cost(4096 * B * 4, 6 << 20),
        name="add_parts",
    )(*parts, after)


def finish_kernel(me_ref, t0, t1, t2, t3, out):
    for k, t in enumerate((t0, t1, t2, t3)):
        out[pl.ds(pl.multiple_of(rel(me_ref[1], -k) * B, B), B), :] = t[...]


def finish_call(me, totals):
    return pl.pallas_call(
        finish_kernel,
        out_shape=jax.ShapeDtypeStruct((512, B), F32),
        in_specs=[SMEM] + [VMEM] * 4,
        out_specs=VMEM,
        compiler_params=params(8),
        cost_estimate=cost(512 * B, 1 << 19),
        name="finish",
    )(me, *totals)


def shift_hid(v, s):
    return lax.ppermute(v, "hid", [(i, (i + s) % HID) for i in range(HID)])


def split_kernel(v1, v3, after, low, high):
    low[...] = v1[...]
    high[...] = v3[...]


def split_call(v1, v3, after):
    half = jax.ShapeDtypeStruct((2048, B), BF16)
    return pl.pallas_call(
        split_kernel,
        out_shape=[half] * 2,
        grid=(1,),
        in_specs=[
            pl.BlockSpec((2048, B), lambda i: (0, 0)),
            pl.BlockSpec((2048, B), lambda i: (1, 0)),
            ANY,
        ],
        out_specs=[pl.BlockSpec((2048, B), lambda i: (0, 0))] * 2,
        compiler_params=params(12),
        cost_estimate=cost(1000, 2 << 20),
        name="halves",
    )(v1, v3, after)


def gather_hid(v, after):
    v1, v3 = shift_hid(v, 1), shift_hid(v, 3)
    low, high = split_call(v1, v3, after)
    return v, v1, shift_hid(low, 1), shift_hid(high, 3), v3


def shift_dom(v, dz, dy, dc):
    pairs = [
        ((z * 4 + y) * 2 + c, (((z + dz) % 8) * 4 + (y + dy) % 4) * 2 + (c ^ dc))
        for z in range(8)
        for y in range(4)
        for c in range(2)
    ]
    return lax.ppermute(v, "dom", pairs)


def swap_z(v, k):
    return lax.ppermute(v, "dom", [(i, i ^ (8 * k)) for i in range(64)])


def all_to_all(v):
    return lax.all_to_all(v, "dom", split_axis=0, concat_axis=0, tiled=True)


def per_device(x, w, tiles, rows, cols, count, send, bits, cot):
    hid = lax.axis_index("hid").astype(jnp.int32)
    dom = lax.axis_index("dom").astype(jnp.int32)
    z, y = dom // 8, (dom // 2) % 4
    me = jnp.stack([hid, y, z])
    bits_t = bits.T

    own, slots = tiles_bwd_call(count, rows, cols, bits_t, cot, tiles)
    returned = all_to_all(slots)

    xs = gather_hid(x, slots)
    mask, ready = active_call(bits_t)
    hidden, outgoing = hidden_call(me, send, xs, w, ready)
    incoming = all_to_all(outgoing)

    terms, p0, p1, p2a, p2b, p3 = sum_call(me, send, own, returned, xs, w, outgoing)

    terms = (terms + shift_dom(terms, 0, 0, 1)).reshape(4, B, B)
    terms = [terms[0]] + [shift_dom(terms[k], 0, k, 0) for k in (1, 3, 2)]
    part = add_call(terms)

    p1, p3 = relay_call(p1, p3, shift_hid(p2a, 1), shift_hid(p2b, 3), part)
    parts = [p0, shift_hid(p1, 1), shift_hid(p3, 3)]

    total = add_z_call(me, [part] + [swap_z(part, k) for k in (1, 2, 3)])
    out_act, token = tiles_fwd_call(count, rows, cols, mask, hidden, incoming, tiles)
    total = pair_call(total, swap_z(total, 4), token)
    weight_grad = finish_call(me, [total] + [shift_dom(total, 0, k, 0) for k in range(1, 4)])
    input_grad = parts_call(parts, total)
    return out_act.reshape(4096, B), input_grad, weight_grad


def solution(mesh):
    placed = (
        P("dom", "hid"),
        P(None, "hid"),
        P("dom", None, None),
        P("dom", None),
        P("dom", None),
        P("dom"),
        P("dom", None),
        P("dom", "hid"),
        P("dom", "hid"),
    )
    return jax.shard_map(
        per_device,
        mesh=mesh,
        in_specs=placed,
        out_specs=(P("dom", "hid"), P("dom", "hid"), P(None, "hid")),
        check_vma=False,
    )
```
